32 devices in a mesh: wall: 4 (over z), span: 8 (over y, x, core).
Axes of the slice: x: 2, y: 2, z: 4, core: 2. Of those that a mesh axis runs over, the one named last changes fastest.
Arguments:
- solution: float32 [5, 125, 8192], P(None, None, ('wall', 'span')), may hold values from -6 to 6
- level_map: int32 [8192], P(('wall', 'span')), may hold values from 0 to 3, as said below
- send_list: int32 [32, 256], P(('wall', 'span')), may hold values from 0 to 1535, as said below
- face_partner: int32 [6, 8192], P(None, ('wall', 'span')), may hold values from 0 to 1791, as said below
- volume_block: float32 [125, 125], replicated
- lift_block: float32 [125, 150], replicated, may hold values from -0.5 to 0.5
- flux_mixing: float32 [5, 5], replicated
- metric_scale: float32 [8192], P(('wall', 'span')), may hold values from 0.5 to 2
Outputs:
- advanced_solution: float32 [5, 125, 8192], P(None, None, ('wall', 'span'))
The draws below stay inside these ranges and needn't reach their ends.
Inputs may be any that keep to these rules, and one draw needn't show every extreme that they name: `level_map`: each partition holds elements of every level. `send_list`: slot k (of 8) from any sender to any receiver names a face of a sender's element of level max(3 - j, 0), where j is the largest whole number with 2**j * (8 - k) <= 8. `face_partner`: in each partition's 256 elements, every column of the received traces is named by exactly one face; the other faces name columns of the partition's own trace table.
All inputs are finite; a program needn't handle non-finite values.
Results may differ from the reference program's by a relative error of at most 0.0001.
Values sent between devices are 32-bit elements; how exact they have to be, the bound alone decides.
A program may use at most 64 MiB of HBM per device.

```python
import math
import jax
import jax.numpy as jnp
import numpy as np
from jax import lax

VARIABLES = 5
DEGREE = 4
NODES = 125
FACE_NODES = 25
TRACE_ROWS = 125
LEVELS = 4
COARSE_STEPS = 3
SLOT_COUNT = 8
DEV_ELEMENTS = 256
PARTITIONS = 32
WALL_PARTS = 4
SPAN_PARTS = 8
ELEMENTS = 8192


def slot_level_of(slot_index):
    power = 0
    while power < LEVELS - 1 and 2 ** (power + 1) * (SLOT_COUNT - slot_index) <= SLOT_COUNT:
        power = power + 1
    return max(LEVELS - 1 - power, 0)


def common_levels(key):
    level_key = jax.random.fold_in(key, 101)
    raw_level = jax.random.randint(jax.random.fold_in(level_key, 1), (ELEMENTS,), 0, 8)
    device = jnp.arange(ELEMENTS) // DEV_ELEMENTS
    wall_row = device // SPAN_PARTS
    offset = 6 * (WALL_PARTS - 1 - wall_row) // max(WALL_PARTS - 1, 1)
    levels = jnp.minimum((raw_level + offset) // 3, LEVELS - 1).astype(jnp.int32)
    levels = levels.reshape(PARTITIONS, DEV_ELEMENTS)

    def force_all(position, row):
        spots = jax.random.permutation(jax.random.fold_in(jax.random.fold_in(level_key, 2), position), DEV_ELEMENTS)[:LEVELS]
        return row.at[spots].set(jnp.arange(LEVELS, dtype=jnp.int32))
    levels = jax.vmap(force_all)(jnp.arange(PARTITIONS), levels)
    return levels.reshape(ELEMENTS).astype(jnp.int32)


def draw_level_map(key, part):
    return common_levels(key)


def draw_send_list(key, part):
    levels = common_levels(key).reshape(PARTITIONS, DEV_ELEMENTS)
    slot_table = jnp.asarray(np.array([slot_level_of(k) for k in range(SLOT_COUNT)] * PARTITIONS, dtype=np.int32))
    send_key = jax.random.fold_in(key, 202)

    def one_sender(position):
        row = levels[position]
        marks = (row[None, :] == jnp.arange(LEVELS, dtype=jnp.int32)[:, None]).astype(jnp.int32)
        running = jnp.cumsum(marks, axis=1)
        counts = running[:, -1]
        subkey = jax.random.fold_in(send_key, position)
        picks = jax.random.randint(jax.random.fold_in(subkey, 1), (PARTITIONS * SLOT_COUNT,), 0, 1 << 20)
        picks = picks % counts[slot_table]
        chosen_running = running[slot_table]
        element = jnp.sum((chosen_running < (picks + 1)[:, None]).astype(jnp.int32), axis=1)
        face = jax.random.randint(jax.random.fold_in(subkey, 2), (PARTITIONS * SLOT_COUNT,), 0, 6)
        return (face * DEV_ELEMENTS + element).astype(jnp.int32)
    return lax.map(one_sender, jnp.arange(PARTITIONS)).astype(jnp.int32)


def draw_face_partner(key, part):
    local_faces = 6 * DEV_ELEMENTS
    remote = PARTITIONS * SLOT_COUNT

    def one_partition(position):
        subkey = jax.random.fold_in(key, position)
        shuffle = jax.random.permutation(jax.random.fold_in(subkey, 1), local_faces)
        local_refs = jax.random.randint(jax.random.fold_in(subkey, 2), (local_faces,), 0, local_faces)
        ranks = jnp.arange(local_faces)
        values = jnp.where(ranks < remote, local_faces + ranks, local_refs).astype(jnp.int32)
        return jnp.zeros((local_faces,), jnp.int32).at[shuffle].set(values)
    pointer_grid = jax.vmap(one_partition)(jnp.arange(PARTITIONS))
    return pointer_grid.reshape(PARTITIONS, 6, DEV_ELEMENTS).transpose(1, 0, 2).reshape(6, ELEMENTS).astype(jnp.int32)


def dominant_block(key, order, weight):
    noise = jax.random.normal(key, (order, order), jnp.float32)
    return jnp.eye(order, dtype=jnp.float32) + weight * noise / math.sqrt(order)


def draw_volume_block(key, part):
    return dominant_block(jax.random.fold_in(key, 11), NODES, 0.3)


def draw_flux_mixing(key, part):
    return dominant_block(jax.random.fold_in(key, 17), VARIABLES, 0.4)


def shard_levels(stream_key, shape, cuts, least, high):
    def one(dim, shards_of):
        steps = jax.random.uniform(jax.random.fold_in(jax.random.fold_in(stream_key, 6), dim), (shards_of,), jnp.float32, least / len(cuts), high / len(cuts))
        return jnp.repeat(jnp.exp(steps), shape[dim] // shards_of).reshape((-1,) + (1,) * (len(shape) - dim - 1))

    gain = one(*cuts[0])
    for cut in cuts[1:]:
        gain = gain * one(*cut)
    return gain


def gaussian(stream_key, extent, deviation, limit, cuts=(), held_as=jnp.bfloat16):
    factor_of = shard_levels(stream_key, extent, cuts, -0.22, 0.18) if cuts else 1.0
    result = jax.random.normal(stream_key, extent, jnp.float32) * deviation * factor_of
    return jnp.minimum(jnp.maximum(result, -limit), limit).astype(held_as)


def setup_inputs(seed: int = 0) -> dict:
    key_of = jax.random.split(jax.random.key(seed), 9)
    return {
        "solution": gaussian(key_of[0], (VARIABLES, NODES, ELEMENTS), 1.0, 6.0, ((2, 32),), jnp.float32),
        "level_map": draw_level_map(jax.random.fold_in(key_of[8], 71), 0),
        "send_list": draw_send_list(jax.random.fold_in(key_of[8], 71), 0),
        "face_partner": draw_face_partner(jax.random.fold_in(key_of[8], 71), 0),
        "volume_block": draw_volume_block(jax.random.fold_in(key_of[8], 71), 0),
        "lift_block": gaussian(key_of[5], (NODES, 6 * FACE_NODES), (6 * FACE_NODES) ** -0.5, 0.5, (), jnp.float32),
        "flux_mixing": draw_flux_mixing(jax.random.fold_in(key_of[8], 71), 0),
        "metric_scale": jnp.clip(jnp.exp(math.log(2.0) - 1.3862944 * jax.random.uniform(key_of[7], (ELEMENTS,), jnp.float32) ** shard_levels(key_of[7], (ELEMENTS,), ((0, 32),), -0.2, 0.2)), 0.5, 2.0),
    }


COURANT = 0.6

def face_traces(fields):
    local_count = fields.shape[2]
    node_cube = fields.reshape(VARIABLES, DEGREE + 1, DEGREE + 1, DEGREE + 1, local_count)
    face_list = [node_cube[:, 0], node_cube[:, -1], node_cube[:, :, 0], node_cube[:, :, -1], node_cube[:, :, :, 0], node_cube[:, :, :, -1]]
    return jnp.stack([face.reshape(VARIABLES, FACE_NODES, local_count) for face in face_list], axis=1)

def tendency(fields, nearby, volume_block, lift_block, flux_mixing, metric_scale):
    local_count = fields.shape[2]
    own_trace = face_traces(fields).reshape(VARIABLES, 6 * FACE_NODES, local_count)
    face_jumps = nearby - own_trace
    combined = jnp.einsum('pj,vje->vpe', lift_block, face_jumps, precision=lax.Precision.HIGHEST)
    combined = combined - jnp.einsum('pq,vqe->vpe', volume_block, fields, precision=lax.Precision.HIGHEST)
    return metric_scale * jnp.einsum('vw,wpe->vpe', flux_mixing, combined, precision=lax.Precision.HIGHEST)

def take_columns(matrix, columns):
    return jnp.take(matrix, columns, axis=1)

def neighbours(fields, send_list, face_partner):
    traces = face_traces(fields)
    trace_table = traces.reshape(VARIABLES, 6, FACE_NODES, PARTITIONS, DEV_ELEMENTS).transpose(3, 0, 2, 1, 4)
    trace_table = trace_table.reshape(PARTITIONS, TRACE_ROWS, 6 * DEV_ELEMENTS)
    outgoing = jax.vmap(take_columns)(trace_table, send_list)
    received = outgoing.reshape(PARTITIONS, TRACE_ROWS, PARTITIONS, SLOT_COUNT).transpose(2, 1, 0, 3)
    received = received.reshape(PARTITIONS, TRACE_ROWS, PARTITIONS * SLOT_COUNT)
    lookup = jnp.concatenate([trace_table, received], axis=2)
    pointers = face_partner.reshape(6, PARTITIONS, DEV_ELEMENTS).transpose(1, 0, 2).reshape(PARTITIONS, 6 * DEV_ELEMENTS)
    gathered = jax.vmap(take_columns)(lookup, pointers)
    gathered = gathered.reshape(PARTITIONS, VARIABLES, FACE_NODES, 6, DEV_ELEMENTS).transpose(1, 3, 2, 0, 4)
    return gathered.reshape(VARIABLES, 6 * FACE_NODES, PARTITIONS * DEV_ELEMENTS)

def lowest_level(substep):
    for candidate in range(LEVELS):
        if substep % 2 ** (LEVELS - 1 - candidate) == 0:
            return candidate
    return LEVELS - 1

def reference(solution, level_map, send_list, face_partner, volume_block, lift_block, flux_mixing, metric_scale):
    fields = solution
    divisors = jnp.power(2, level_map).astype(jnp.float32)
    for coarse in range(COARSE_STEPS):
        element_rates = metric_scale * (1.0 + jnp.sqrt(lax.optimization_barrier(jnp.mean(fields * fields, axis=(0, 1)))))
        coarse_dt = COURANT / jnp.max(element_rates)
        step_sizes = coarse_dt / divisors
        for substep in range(2 ** (LEVELS - 1)):
            lowest = lowest_level(substep)
            nearby = neighbours(fields, send_list, face_partner)
            change = tendency(fields, nearby, volume_block, lift_block, flux_mixing, metric_scale)
            fields = fields + jnp.where(level_map >= lowest, step_sizes * change, 0.0)
    return fields
```

```python
import functools

import jax
import jax.numpy as jnp
import ml_dtypes
import numpy as np
from jax import lax
from jax.experimental import pallas as pl
from jax.experimental.pallas import tpu as pltpu
from jax.sharding import PartitionSpec as P

VARIABLES = 5
DEGREE = 4
NODES = 125
FACE_NODES = 25
FACES = 6
LEVELS = 4
COARSE_STEPS = 3
SUBSTEPS = 2 ** (LEVELS - 1)
COURANT = 0.6

GROUPS = 4
GROUP = 32
SPARE = GROUP - FACE_NODES
ROWS = GROUPS * GROUP
STACK = FACES * GROUP
RATE_ROW = ROWS - 1
PAD = 128
LAST = VARIABLES - 1

BF16 = jnp.bfloat16
F32 = jnp.float32


def face_nodes():
    cube = np.arange(NODES).reshape(5, 5, 5)
    faces = [cube[0], cube[-1], cube[:, 0], cube[:, -1], cube[:, :, 0], cube[:, :, -1]]
    return np.stack([face.reshape(-1) for face in faces])


def index_blocks():
    nodes = face_nodes()
    pick = np.zeros((GROUPS, STACK, 2 * PAD), np.float32)
    spread = np.zeros((2 * PAD, (GROUPS + 1) * STACK), np.float32)
    own = np.zeros((2 * PAD, PAD), np.float32)
    for face in range(FACES):
        for node in range(FACE_NODES):
            source = face * FACE_NODES + node
            own[source, nodes[face, node]] = 1
            spread[source, face * GROUP + node] = 1
            group, place = divmod(node, SPARE)
            slot = face * GROUP + FACE_NODES + place
            spread[source, (1 + group) * STACK + slot] = 1
            pick[group, slot, PAD + nodes[face, node]] = 1
            for g in range(GROUPS):
                pick[g, face * GROUP + node, nodes[face, node]] = 1
    return tuple(x.astype(ml_dtypes.bfloat16) for x in (pick, spread, own))


def split(x):
    high = x.astype(BF16)
    return high, (x - high.astype(F32)).astype(BF16)


def dot(a, b):
    return jnp.dot(a, b, preferred_element_type=F32)


def kernel(
    peers, span, slots,
    x_ref, level_ref, send_ref, partner_ref, volume_ref, lift_ref, flux_ref, metric_ref,
    pick_ref, spread_ref, own_ref,
    out_ref,
    fields, halves, table, route, send_route, near, near_half, change,
    lift_high, lift_low, vol_high, vol_low, wide, coefs, rate,
    outbox, inbox, send_sem, recv_sem,
):
    local = x_ref.shape[2]
    width = peers * slots
    columns = FACES * local
    me = lax.axis_index("wall") * span + lax.axis_index("span")

    def place_of(peer):
        return (peer // span, lax.rem(peer, span))

    barrier = pltpu.get_barrier_semaphore()

    def greet(i, carry):
        pl.semaphore_signal(
            barrier, inc=1, device_id=place_of(lax.rem(me + i, peers)),
            device_id_type=pl.DeviceIdType.MESH,
        )
        return carry

    lax.fori_loop(1, peers, greet, 0)

    def route_rows(i, carry):
        base = pl.multiple_of(i * 256, 256)
        rows = lax.broadcasted_iota(jnp.int32, (256, local), 0) + base
        for face in range(FACES):
            hit = rows == partner_ref[face : face + 1, :]
            route[pl.ds(base, 256), face * local : (face + 1) * local] = jnp.where(
                hit, 1.0, 0.0
            ).astype(BF16)
        return carry

    lax.fori_loop(0, (columns + width) // 256, route_rows, 0)

    def send_rows(i, carry):
        base = pl.multiple_of(i * 256, 256)
        rows = lax.broadcasted_iota(jnp.int32, (256, width), 0) + base
        send_route[pl.ds(base, 256), :] = jnp.where(rows == send_ref[...], 1.0, 0.0).astype(BF16)
        return carry

    lax.fori_loop(0, columns // 256, send_rows, 0)

    wide[...] = jnp.zeros_like(wide)
    wide[0:NODES, 0 : FACES * FACE_NODES] = lift_ref[...]
    wide_high, wide_low = split(wide[...])
    for half, target in ((wide_high, lift_high), (wide_low, lift_low)):
        spread = dot(half, spread_ref[...]).astype(BF16)
        for g in range(GROUPS):
            target[g, 0:PAD, :] = spread[:, 0:STACK]
            target[g, PAD : 2 * PAD, :] = spread[:, (1 + g) * STACK : (2 + g) * STACK]
    own = dot(wide_high, own_ref[...]) + dot(wide_low, own_ref[...])
    wide[...] = jnp.zeros_like(wide)
    wide[0:NODES, 0:NODES] = volume_ref[...]
    high, low = split(wide[:, 0:PAD] + own)
    vol_high[:, 0:PAD] = high
    vol_high[:, PAD : 2 * PAD] = high
    vol_low[...] = low

    fields[...] = jnp.zeros_like(fields)
    for v in range(VARIABLES):
        fields[v, 0:NODES, :] = x_ref[v]
    rate[...] = jnp.zeros_like(rate)

    pl.semaphore_wait(barrier, peers - 1)

    def substep(step, carry):
        phase = lax.rem(step, SUBSTEPS)
        now = lax.rem(step, 2)

        for v in range(VARIABLES):
            high, low = split(fields[v])
            halves[v, 0:PAD, :] = high
            halves[v, PAD : 2 * PAD, :] = low
        for g in range(GROUPS):
            for half in range(2):
                rows = slice(half * PAD, (half + 1) * PAD)
                both = jnp.concatenate([halves[g, rows, :], halves[LAST, rows, :]], axis=0)
                traces = dot(pick_ref[g], both).astype(BF16)
                for face in range(FACES):
                    table[
                        half * ROWS + g * GROUP : half * ROWS + (g + 1) * GROUP,
                        face * local : (face + 1) * local,
                    ] = traces[face * GROUP : (face + 1) * GROUP, :]

        @pl.when(phase == 0)
        def _():
            total = jnp.zeros((1, local), F32)
            for v in range(VARIABLES):
                total = total + jnp.sum(fields[v] * fields[v], axis=0, keepdims=True)
            rates = metric_ref[...] * (1.0 + jnp.sqrt(total * (1.0 / (VARIABLES * NODES))))
            rate[...] = jnp.broadcast_to(jnp.max(rates, axis=1, keepdims=True), rate.shape)

        chosen = dot(table[...], send_route[...])
        chosen = chosen[0:ROWS, :] + chosen[ROWS : 2 * ROWS, :]
        row_ids = lax.broadcasted_iota(jnp.int32, (ROWS, width), 0)
        chosen = jnp.where(row_ids == RATE_ROW, rate[0:1, 0:1], chosen)
        outbox[now] = chosen.T

        def send(i, carry):
            peer = lax.rem(me + i, peers)
            pltpu.make_async_remote_copy(
                src_ref=outbox.at[now, pl.ds(pl.multiple_of(peer * slots, slots), slots)],
                dst_ref=inbox.at[now, pl.ds(pl.multiple_of(me * slots, slots), slots)],
                send_sem=send_sem.at[now],
                recv_sem=recv_sem.at[now],
                device_id=place_of(peer),
                device_id_type=pl.DeviceIdType.MESH,
            ).start()
            return carry

        lax.fori_loop(1, peers, send, 0)
        mine = pl.ds(pl.multiple_of(me * slots, slots), slots)
        inbox[now, mine, :] = outbox[now, mine, :]

        def near_face(face, carry):
            lanes = pl.ds(pl.multiple_of(face * local, local), local)
            near[:, lanes] = dot(table[...], route[0:columns, lanes])
            return carry

        lax.fori_loop(0, FACES, near_face, 0)
        for v in range(VARIABLES):
            change[v] = dot(vol_high[...], halves[v]) + dot(vol_low[...], halves[v, 0:PAD, :])

        bulk = pl.ds(0, (peers - 1) * slots)
        pltpu.make_async_copy(
            inbox.at[now, bulk], inbox.at[now, bulk], recv_sem.at[now]
        ).wait()
        received = inbox[now].T

        @pl.when(phase == 0)
        def _():
            fastest = jnp.max(received[RATE_ROW : RATE_ROW + 1, :], axis=1, keepdims=True)
            divisors = jnp.left_shift(1, level_ref[...]).astype(F32)
            coefs[...] = COURANT / fastest / divisors

        received = jnp.where(row_ids == RATE_ROW, 0.0, received)
        high, low = split(received)
        received = jnp.concatenate([high, low], axis=0)

        for face in range(FACES):
            lanes = slice(face * local, (face + 1) * local)
            total = near[:, lanes] + dot(received, route[columns : columns + width, lanes])
            near_half[:, lanes] = total.astype(BF16)

        last = jnp.zeros((PAD, local), F32)
        combined = []
        for g in range(GROUPS):
            parts = []
            for half in range(2):
                rows = slice(half * ROWS + g * GROUP, half * ROWS + (g + 1) * GROUP)
                parts.append(
                    jnp.concatenate(
                        [near_half[rows, f * local : (f + 1) * local] for f in range(FACES)],
                        axis=0,
                    )
                )
            lifted = dot(lift_high[g], parts[0])
            lifted = lifted + dot(lift_low[g], parts[0])
            lifted = lifted + dot(lift_high[g], parts[1])
            combined.append(lifted[0:PAD, :] - change[g])
            last = last + lifted[PAD : 2 * PAD, :]
        combined.append(last - change[LAST])
        for v in range(VARIABLES):
            change[v] = combined[v]

        lowest = jnp.where(
            phase == 0, 0, jnp.where(lax.rem(phase, 4) == 0, 1, jnp.where(lax.rem(phase, 2) == 0, 2, 3))
        )
        scale = jnp.where(level_ref[...] >= lowest, coefs[...], 0.0) * metric_ref[...]
        for v in range(VARIABLES):
            mixed = flux_ref[v, 0] * change[0]
            for w in range(1, VARIABLES):
                mixed = mixed + flux_ref[v, w] * change[w]
            fields[v] = fields[v] + scale * mixed

        pltpu.make_async_copy(
            outbox.at[now, bulk], outbox.at[now, bulk], send_sem.at[now]
        ).wait()
        return carry

    lax.fori_loop(0, COARSE_STEPS * SUBSTEPS, substep, 0)
    for v in range(VARIABLES):
        out_ref[v] = fields[v, 0:NODES, :]


def body(x, level_map, send_list, face_partner, volume_block, lift_block, flux_mixing, metric_scale):
    peers = lax.axis_size(("wall", "span"))
    span = lax.axis_size("span")
    local = x.shape[2]
    width = send_list.shape[1]
    slots = width // peers
    columns = FACES * local
    vmem = pl.BlockSpec(memory_space=pltpu.VMEM)
    smem = pl.BlockSpec(memory_space=pltpu.SMEM)
    pick, spread, own = index_blocks()
    return pl.pallas_call(
        functools.partial(kernel, peers, span, slots),
        out_shape=jax.ShapeDtypeStruct(x.shape, x.dtype),
        in_specs=[vmem] * 6 + [smem] + [vmem] * 4,
        out_specs=vmem,
        scratch_shapes=[
            pltpu.VMEM((VARIABLES, PAD, local), F32),
            pltpu.VMEM((VARIABLES, 2 * PAD, local), BF16),
            pltpu.VMEM((2 * ROWS, columns), BF16),
            pltpu.VMEM((columns + width, columns), BF16),
            pltpu.VMEM((columns, width), BF16),
            pltpu.VMEM((2 * ROWS, columns), F32),
            pltpu.VMEM((2 * ROWS, columns), BF16),
            pltpu.VMEM((VARIABLES, PAD, local), F32),
            pltpu.VMEM((GROUPS, 2 * PAD, STACK), BF16),
            pltpu.VMEM((GROUPS, 2 * PAD, STACK), BF16),
            pltpu.VMEM((PAD, 2 * PAD), BF16),
            pltpu.VMEM((PAD, PAD), BF16),
            pltpu.VMEM((PAD, 2 * PAD), F32),
            pltpu.VMEM((1, local), F32),
            pltpu.VMEM((8, 128), F32),
            pltpu.VMEM((2, width, ROWS), F32),
            pltpu.VMEM((2, width, ROWS), F32),
            pltpu.SemaphoreType.DMA((2,)),
            pltpu.SemaphoreType.DMA((2,)),
        ],
        compiler_params=pltpu.CompilerParams(
            collective_id=0, has_side_effects=True, vmem_limit_bytes=48 * 1024 * 1024
        ),
    )(
        x, level_map.reshape(1, local), send_list, face_partner, volume_block, lift_block,
        flux_mixing, metric_scale.reshape(1, local),
        jnp.asarray(pick), jnp.asarray(spread), jnp.asarray(own),
    )


def solution(mesh):
    both = ("wall", "span")
    return jax.shard_map(
        body,
        mesh=mesh,
        in_specs=(
            P(None, None, both), P(both), P(both, None), P(None, both), P(), P(), P(), P(both),
        ),
        out_specs=P(None, None, both),
        check_vma=False,
    )
```

```python
import functools

import jax
import jax.numpy as jnp
import ml_dtypes
import numpy as np
from jax import lax
from jax.experimental import pallas as pl
from jax.experimental.pallas import tpu as pltpu
from jax.sharding import PartitionSpec as P

VARIABLES = 5
DEGREE = 4
NODES = 125
FACE_NODES = 25
FACES = 6
LEVELS = 4
COARSE_STEPS = 3
SUBSTEPS = 2 ** (LEVELS - 1)
COURANT = 0.6

GROUPS = 4
GROUP = 32
SPARE = GROUP - FACE_NODES
ROWS = GROUPS * GROUP
STACK = FACES * GROUP
RATE_ROW = ROWS - 1
PAD = 128
LAST = VARIABLES - 1

BF16 = jnp.bfloat16
F32 = jnp.float32


def face_nodes():
    cube = np.arange(NODES).reshape(5, 5, 5)
    faces = [cube[0], cube[-1], cube[:, 0], cube[:, -1], cube[:, :, 0], cube[:, :, -1]]
    return np.stack([face.reshape(-1) for face in faces])


def index_blocks():
    nodes = face_nodes()
    pick = np.zeros((GROUPS, STACK, 2 * PAD), np.float32)
    spread = np.zeros((2 * PAD, (GROUPS + 1) * STACK), np.float32)
    own = np.zeros((2 * PAD, PAD), np.float32)
    for face in range(FACES):
        for node in range(FACE_NODES):
            source = face * FACE_NODES + node
            own[source, nodes[face, node]] = 1
            spread[source, face * GROUP + node] = 1
            group, place = divmod(node, SPARE)
            slot = face * GROUP + FACE_NODES + place
            spread[source, (1 + group) * STACK + slot] = 1
            pick[group, slot, PAD + nodes[face, node]] = 1
            for g in range(GROUPS):
                pick[g, face * GROUP + node, nodes[face, node]] = 1
    return tuple(x.astype(ml_dtypes.bfloat16) for x in (pick, spread, own))


def slot_count(slots, lowest):
    def level(k):
        power = 0
        while power < LEVELS - 1 and 2 ** (power + 1) * (slots - k) <= slots:
            power += 1
        return LEVELS - 1 - power

    return sum(level(k) >= lowest for k in range(slots))


def split(x):
    high = x.astype(BF16)
    return high, (x - high.astype(F32)).astype(BF16)


def dot(a, b):
    return jnp.dot(a, b, preferred_element_type=F32)


def kernel(
    peers, span, slots,
    x_ref, level_ref, send_ref, partner_ref, volume_ref, lift_ref, flux_ref, metric_ref,
    pick_ref, spread_ref, own_ref,
    out_ref,
    fields, halves, table, route, send_route, near, near_half, change,
    lift_high, lift_low, vol_high, vol_low, wide, coefs, rate,
    outbox, inbox, kept, send_sem, recv_sem,
):
    local = x_ref.shape[2]
    width = peers * slots
    columns = FACES * local
    me = lax.axis_index("wall") * span + lax.axis_index("span")

    def place_of(peer):
        return (peer // span, lax.rem(peer, span))

    barrier = pltpu.get_barrier_semaphore()

    def greet(i, carry):
        pl.semaphore_signal(
            barrier, inc=1, device_id=place_of(lax.rem(me + i, peers)),
            device_id_type=pl.DeviceIdType.MESH,
        )
        return carry

    lax.fori_loop(1, peers, greet, 0)

    def route_rows(i, carry):
        base = pl.multiple_of(i * 256, 256)
        rows = lax.broadcasted_iota(jnp.int32, (256, local), 0) + base
        for face in range(FACES):
            hit = rows == partner_ref[face : face + 1, :]
            route[pl.ds(base, 256), face * local : (face + 1) * local] = jnp.where(
                hit, 1.0, 0.0
            ).astype(BF16)
        return carry

    lax.fori_loop(0, (columns + width) // 256, route_rows, 0)

    def send_rows(i, carry):
        base = pl.multiple_of(i * 256, 256)
        rows = lax.broadcasted_iota(jnp.int32, (256, width), 0) + base
        send_route[pl.ds(base, 256), :] = jnp.where(rows == send_ref[...], 1.0, 0.0).astype(BF16)
        return carry

    lax.fori_loop(0, columns // 256, send_rows, 0)

    wide[...] = jnp.zeros_like(wide)
    wide[0:NODES, 0 : FACES * FACE_NODES] = lift_ref[...]
    wide_high, wide_low = split(wide[...])
    for half, target in ((wide_high, lift_high), (wide_low, lift_low)):
        spread = dot(half, spread_ref[...]).astype(BF16)
        for g in range(GROUPS):
            target[g, 0:PAD, :] = spread[:, 0:STACK]
            target[g, PAD : 2 * PAD, :] = spread[:, (1 + g) * STACK : (2 + g) * STACK]
    own = dot(wide_high, own_ref[...]) + dot(wide_low, own_ref[...])
    wide[...] = jnp.zeros_like(wide)
    wide[0:NODES, 0:NODES] = volume_ref[...]
    high, low = split(wide[:, 0:PAD] + own)
    vol_high[:, 0:PAD] = high
    vol_high[:, PAD : 2 * PAD] = high
    vol_low[...] = low

    fields[...] = jnp.zeros_like(fields)
    for v in range(VARIABLES):
        fields[v, 0:NODES, :] = x_ref[v]
    rate[...] = jnp.zeros_like(rate)
    kept[...] = jnp.zeros_like(kept)

    pl.semaphore_wait(barrier, peers - 1)

    walls = peers // span
    my_wall, my_span = lax.axis_index("wall"), lax.axis_index("span")
    order = []
    for ahead in sorted(range(walls), key=lambda w: -min(w, walls - w)):
        wall = my_wall + ahead
        wall = jnp.where(wall >= walls, wall - walls, wall)
        for beside in range(span):
            if ahead or beside:
                other = my_span + beside
                order.append((wall, jnp.where(other >= span, other - span, other)))

    fine, middle = slot_count(slots, LEVELS - 1), slot_count(slots, LEVELS - 2)

    def sends(step, phase):
        first = step == 0
        odd = lax.rem(phase, 2) == 1
        part = jnp.logical_and(odd, lax.rem(phase, 4) == 3)
        whole = jnp.logical_or(first, jnp.logical_and(odd, lax.rem(phase, 4) == 1))
        few = jnp.logical_and(lax.rem(phase, 2) == 0, step > 0)
        return ((fine, few), (middle, part), (slots, whole))

    def substep(step, carry):
        phase = lax.rem(step, SUBSTEPS)
        now = lax.rem(step, 2)

        for v in range(VARIABLES):
            high, low = split(fields[v])
            halves[v, 0:PAD, :] = high
            halves[v, PAD : 2 * PAD, :] = low
        for g in range(GROUPS):
            for half in range(2):
                rows = slice(half * PAD, (half + 1) * PAD)
                both = jnp.concatenate([halves[g, rows, :], halves[LAST, rows, :]], axis=0)
                traces = dot(pick_ref[g], both).astype(BF16)
                for face in range(FACES):
                    table[
                        half * ROWS + g * GROUP : half * ROWS + (g + 1) * GROUP,
                        face * local : (face + 1) * local,
                    ] = traces[face * GROUP : (face + 1) * GROUP, :]

        @pl.when(phase == 0)
        def _():
            total = jnp.zeros((1, local), F32)
            for v in range(VARIABLES):
                total = total + jnp.sum(fields[v] * fields[v], axis=0, keepdims=True)
            rates = metric_ref[...] * (1.0 + jnp.sqrt(total * (1.0 / (VARIABLES * NODES))))
            rate[...] = jnp.broadcast_to(jnp.max(rates, axis=1, keepdims=True), rate.shape)

        chosen = dot(table[...], send_route[...])
        chosen = chosen[0:ROWS, :] + chosen[ROWS : 2 * ROWS, :]
        row_ids = lax.broadcasted_iota(jnp.int32, (ROWS, width), 0)
        chosen = jnp.where(row_ids == RATE_ROW, rate[0:1, 0:1], chosen)
        outbox[now] = chosen.T

        for count, chosen_now in sends(step, phase):

            @pl.when(chosen_now)
            def _(count=count):
                for there in order:
                    peer = there[0] * span + there[1]
                    pltpu.make_async_remote_copy(
                        src_ref=outbox.at[now, pl.ds(pl.multiple_of(peer * slots, slots), count)],
                        dst_ref=inbox.at[now, pl.ds(pl.multiple_of(me * slots, slots), count)],
                        send_sem=send_sem.at[now],
                        recv_sem=recv_sem.at[now],
                        device_id=there,
                        device_id_type=pl.DeviceIdType.MESH,
                    ).start()

        mine = pl.ds(pl.multiple_of(me * slots, slots), slots)
        inbox[now, mine, :] = outbox[now, mine, :]

        def near_face(face, carry):
            lanes = pl.ds(pl.multiple_of(face * local, local), local)
            near[:, lanes] = dot(table[...], route[0:columns, lanes])
            return carry

        lax.fori_loop(0, FACES, near_face, 0)
        for v in range(VARIABLES):
            change[v] = dot(vol_high[...], halves[v]) + dot(vol_low[...], halves[v, 0:PAD, :])

        for count, chosen_now in sends(step, phase):

            @pl.when(chosen_now)
            def _(count=count):
                bulk = inbox.at[now, pl.ds(0, (peers - 1) * count)]
                pltpu.make_async_copy(bulk, bulk, recv_sem.at[now]).wait()

        lane_ids = lax.broadcasted_iota(jnp.int32, (ROWS, width), 1)
        finest = lax.rem(lane_ids, slots) < slot_count(slots, LEVELS - 1)
        brought = jnp.where(jnp.logical_or(now == 1, step == 0), slots, 0)
        received = jnp.where(
            jnp.logical_or(finest, lax.rem(lane_ids, slots) < brought), inbox[now].T, kept[...]
        )
        kept[...] = received

        @pl.when(phase == 0)
        def _():
            fresh = jnp.where(finest[0:1, :], received[RATE_ROW : RATE_ROW + 1, :], 0.0)
            fastest = jnp.max(fresh, axis=1, keepdims=True)
            divisors = jnp.left_shift(1, level_ref[...]).astype(F32)
            coefs[...] = COURANT / fastest / divisors

        received = jnp.where(row_ids == RATE_ROW, 0.0, received)
        high, low = split(received)
        received = jnp.concatenate([high, low], axis=0)

        for face in range(FACES):
            lanes = slice(face * local, (face + 1) * local)
            total = near[:, lanes] + dot(received, route[columns : columns + width, lanes])
            near_half[:, lanes] = total.astype(BF16)

        last = jnp.zeros((PAD, local), F32)
        combined = []
        for g in range(GROUPS):
            parts = []
            for half in range(2):
                rows = slice(half * ROWS + g * GROUP, half * ROWS + (g + 1) * GROUP)
                parts.append(
                    jnp.concatenate(
                        [near_half[rows, f * local : (f + 1) * local] for f in range(FACES)],
                        axis=0,
                    )
                )
            lifted = dot(lift_high[g], parts[0])
            lifted = lifted + dot(lift_low[g], parts[0])
            lifted = lifted + dot(lift_high[g], parts[1])
            combined.append(lifted[0:PAD, :] - change[g])
            last = last + lifted[PAD : 2 * PAD, :]
        combined.append(last - change[LAST])
        for v in range(VARIABLES):
            change[v] = combined[v]

        lowest = jnp.where(
            phase == 0, 0, jnp.where(lax.rem(phase, 4) == 0, 1, jnp.where(lax.rem(phase, 2) == 0, 2, 3))
        )
        scale = jnp.where(level_ref[...] >= lowest, coefs[...], 0.0) * metric_ref[...]
        for v in range(VARIABLES):
            mixed = flux_ref[v, 0] * change[0]
            for w in range(1, VARIABLES):
                mixed = mixed + flux_ref[v, w] * change[w]
            fields[v] = fields[v] + scale * mixed

        for count, chosen_now in sends(step, phase):

            @pl.when(chosen_now)
            def _(count=count):
                bulk = outbox.at[now, pl.ds(0, (peers - 1) * count)]
                pltpu.make_async_copy(bulk, bulk, send_sem.at[now]).wait()

        return carry

    lax.fori_loop(0, COARSE_STEPS * SUBSTEPS, substep, 0)
    for v in range(VARIABLES):
        out_ref[v] = fields[v, 0:NODES, :]


def body(x, level_map, send_list, face_partner, volume_block, lift_block, flux_mixing, metric_scale):
    peers = lax.axis_size(("wall", "span"))
    span = lax.axis_size("span")
    local = x.shape[2]
    width = send_list.shape[1]
    slots = width // peers
    columns = FACES * local
    vmem = pl.BlockSpec(memory_space=pltpu.VMEM)
    smem = pl.BlockSpec(memory_space=pltpu.SMEM)
    pick, spread, own = index_blocks()
    return pl.pallas_call(
        functools.partial(kernel, peers, span, slots),
        out_shape=jax.ShapeDtypeStruct(x.shape, x.dtype),
        in_specs=[vmem] * 6 + [smem] + [vmem] * 4,
        out_specs=vmem,
        scratch_shapes=[
            pltpu.VMEM((VARIABLES, PAD, local), F32),
            pltpu.VMEM((VARIABLES, 2 * PAD, local), BF16),
            pltpu.VMEM((2 * ROWS, columns), BF16),
            pltpu.VMEM((columns + width, columns), BF16),
            pltpu.VMEM((columns, width), BF16),
            pltpu.VMEM((2 * ROWS, columns), F32),
            pltpu.VMEM((2 * ROWS, columns), BF16),
            pltpu.VMEM((VARIABLES, PAD, local), F32),
            pltpu.VMEM((GROUPS, 2 * PAD, STACK), BF16),
            pltpu.VMEM((GROUPS, 2 * PAD, STACK), BF16),
            pltpu.VMEM((PAD, 2 * PAD), BF16),
            pltpu.VMEM((PAD, PAD), BF16),
            pltpu.VMEM((PAD, 2 * PAD), F32),
            pltpu.VMEM((1, local), F32),
            pltpu.VMEM((8, 128), F32),
            pltpu.VMEM((2, width, ROWS), F32),
            pltpu.VMEM((2, width, ROWS), F32),
            pltpu.VMEM((ROWS, width), F32),
            pltpu.SemaphoreType.DMA((2,)),
            pltpu.SemaphoreType.DMA((2,)),
        ],
        compiler_params=pltpu.CompilerParams(
            collective_id=0, has_side_effects=True, vmem_limit_bytes=48 * 1024 * 1024
        ),
    )(
        x, level_map.reshape(1, local), send_list, face_partner, volume_block, lift_block,
        flux_mixing, metric_scale.reshape(1, local),
        jnp.asarray(pick), jnp.asarray(spread), jnp.asarray(own),
    )


def solution(mesh):
    both = ("wall", "span")
    return jax.shard_map(
        body,
        mesh=mesh,
        in_specs=(
            P(None, None, both), P(both), P(both, None), P(None, both), P(), P(), P(), P(both),
        ),
        out_specs=P(None, None, both),
        check_vma=False,
    )
```

```python
import functools

import jax
import jax.numpy as jnp
import ml_dtypes
import numpy as np
from jax import lax
from jax.experimental import pallas as pl
from jax.experimental.pallas import tpu as pltpu
from jax.sharding import PartitionSpec as P

VARIABLES = 5
DEGREE = 4
NODES = 125
FACE_NODES = 25
FACES = 6
LEVELS = 4
COARSE_STEPS = 3
SUBSTEPS = 2 ** (LEVELS - 1)
COURANT = 0.6

GROUPS = 4
GROUP = 32
SPARE = GROUP - FACE_NODES
ROWS = GROUPS * GROUP
STACK = FACES * GROUP
RATE_ROW = ROWS - 1
SPREAD = 4
CHUNK = 16
PAD = 128
LAST = VARIABLES - 1

BF16 = jnp.bfloat16
F32 = jnp.float32


def face_nodes():
    cube = np.arange(NODES).reshape(5, 5, 5)
    faces = [cube[0], cube[-1], cube[:, 0], cube[:, -1], cube[:, :, 0], cube[:, :, -1]]
    return np.stack([face.reshape(-1) for face in faces])


def index_blocks():
    nodes = face_nodes()
    pick = np.zeros((GROUPS, STACK, 2 * PAD), np.float32)
    spread = np.zeros((2 * PAD, (GROUPS + 1) * STACK), np.float32)
    own = np.zeros((2 * PAD, PAD), np.float32)
    for face in range(FACES):
        for node in range(FACE_NODES):
            source = face * FACE_NODES + node
            own[source, nodes[face, node]] = 1
            spread[source, face * GROUP + node] = 1
            group, place = divmod(node, SPARE)
            slot = face * GROUP + FACE_NODES + place
            spread[source, (1 + group) * STACK + slot] = 1
            pick[group, slot, PAD + nodes[face, node]] = 1
            for g in range(GROUPS):
                pick[g, face * GROUP + node, nodes[face, node]] = 1
    wide = np.zeros((2 * PAD, SPREAD * 2 * PAD), np.float32)
    wide[:, : spread.shape[1]] = spread
    blocks = [pick.reshape(GROUPS * STACK, 2 * PAD)]
    blocks += [wide[:, i * 2 * PAD : (i + 1) * 2 * PAD] for i in range(SPREAD)]
    blocks.append(np.pad(own, ((0, 0), (0, PAD))))
    return np.concatenate(blocks).astype(ml_dtypes.bfloat16)


def slot_count(slots, lowest):
    def level(k):
        power = 0
        while power < LEVELS - 1 and 2 ** (power + 1) * (slots - k) <= slots:
            power += 1
        return LEVELS - 1 - power

    return sum(level(k) >= lowest for k in range(slots))


def split(x):
    high = x.astype(BF16)
    return high, (x - high.astype(F32)).astype(BF16)


def dot(a, b):
    return jnp.dot(a, b, preferred_element_type=F32)


def kernel(
    peers, span, slots,
    x_ref, level_ref, send_ref, partner_ref, volume_ref, lift_ref, flux_ref, metric_ref,
    index_ref,
    out_ref,
    fields, halves, table, route, send_route, near, near_half, change, lifted,
    lift_wide, vol_wide, wide, tall, coefs, rate, index,
    outbox, inbox, kept, send_sem, recv_sem, index_sem,
):
    local = x_ref.shape[2]
    width = peers * slots
    columns = FACES * local
    me = lax.axis_index("wall") * span + lax.axis_index("span")

    def place_of(peer):
        return (peer // span, lax.rem(peer, span))

    index_copy = pltpu.make_async_copy(index_ref, index, index_sem)
    index_copy.start()
    barrier = pltpu.get_barrier_semaphore()

    def greet(i, carry):
        pl.semaphore_signal(
            barrier, inc=1, device_id=place_of(lax.rem(me + i, peers)),
            device_id_type=pl.DeviceIdType.MESH,
        )
        return carry

    lax.fori_loop(1, peers, greet, 0)

    def route_rows(i, carry):
        base = pl.multiple_of(i * 256, 256)
        rows = lax.broadcasted_iota(jnp.int32, (256, local), 0) + base
        for face in range(FACES):
            hit = rows == partner_ref[face : face + 1, :]
            route[pl.ds(base, 256), face * local : (face + 1) * local] = jnp.where(
                hit, 1.0, 0.0
            ).astype(BF16)
        return carry

    lax.fori_loop(0, (columns + width) // 256, route_rows, 0)

    def send_rows(i, carry):
        base = pl.multiple_of(i * 256, 256)
        rows = lax.broadcasted_iota(jnp.int32, (256, width), 0) + base
        send_route[pl.ds(base, 256), :] = jnp.where(rows == send_ref[...], 1.0, 0.0).astype(BF16)
        return carry

    lax.fori_loop(0, columns // 256, send_rows, 0)

    tall[...] = jnp.zeros_like(tall)
    tall[0 : FACES * FACE_NODES, 0:NODES] = lift_ref[...]
    index_copy.wait()
    wide_halves = split(tall[...].T)
    first = GROUPS * STACK
    for place, half in ((0, 0), (1, 1), (2, 0)):
        spread = jnp.concatenate(
            [
                dot(wide_halves[half], index[first + i * 2 * PAD : first + (i + 1) * 2 * PAD, :])
                for i in range(SPREAD)
            ],
            axis=1,
        ).astype(BF16)
        lanes = slice(place * STACK, (place + 1) * STACK)
        for g in range(GROUPS):
            lift_wide[g, 0:PAD, lanes] = spread[:, 0:STACK]
            lift_wide[g, PAD : 2 * PAD, lanes] = spread[:, (1 + g) * STACK : (2 + g) * STACK]
    own_ref = index[first + SPREAD * 2 * PAD :, 0:PAD]
    own = dot(wide_halves[0], own_ref) + dot(wide_halves[1], own_ref)
    wide[...] = jnp.zeros_like(wide)
    wide[0:NODES, 0:NODES] = volume_ref[...]
    high, low = split(wide[...] + own)
    vol_wide[:, 0:PAD] = high
    vol_wide[:, PAD : 2 * PAD] = high
    vol_wide[:, 2 * PAD : 3 * PAD] = low

    fields[...] = jnp.zeros_like(fields)
    for v in range(VARIABLES):
        fields[v, 0:NODES, :] = x_ref[v]
        high, low = split(fields[v])
        halves[v, 0:PAD, :] = high
        halves[v, PAD : 2 * PAD, :] = low
    rate[...] = jnp.zeros_like(rate)
    kept[...] = jnp.zeros_like(kept)

    pl.semaphore_wait(barrier, peers - 1)

    walls = peers // span
    my_wall, my_span = lax.axis_index("wall"), lax.axis_index("span")
    order = []
    for ahead in sorted(range(walls), key=lambda w: -min(w, walls - w)):
        wall = my_wall + ahead
        wall = jnp.where(wall >= walls, wall - walls, wall)
        for beside in range(span):
            if ahead or beside:
                other = my_span + beside
                order.append((wall, jnp.where(other >= span, other - span, other)))

    fine, middle = slot_count(slots, LEVELS - 1), slot_count(slots, LEVELS - 2)

    def sends(step, phase):
        first = step == 0
        odd = lax.rem(phase, 2) == 1
        part = jnp.logical_and(odd, lax.rem(phase, 4) == 3)
        whole = jnp.logical_or(first, jnp.logical_and(odd, lax.rem(phase, 4) == 1))
        few = jnp.logical_and(lax.rem(phase, 2) == 0, step > 0)
        return ((fine, few), (middle, part), (slots, whole))

    def substep(step, carry):
        phase = lax.rem(step, SUBSTEPS)
        now = lax.rem(step, 2)

        for g in range(GROUPS):
            for half in range(2):
                rows = slice(half * PAD, (half + 1) * PAD)
                both = jnp.concatenate([halves[g, rows, :], halves[LAST, rows, :]], axis=0)
                traces = dot(index[g * STACK : (g + 1) * STACK, :], both).astype(BF16)
                for face in range(FACES):
                    table[
                        half * ROWS + g * GROUP : half * ROWS + (g + 1) * GROUP,
                        face * local : (face + 1) * local,
                    ] = traces[face * GROUP : (face + 1) * GROUP, :]

        @pl.when(phase == 0)
        def _():
            total = jnp.zeros((1, local), F32)
            for v in range(VARIABLES):
                total = total + jnp.sum(fields[v] * fields[v], axis=0, keepdims=True)
            rates = metric_ref[...] * (1.0 + jnp.sqrt(total * (1.0 / (VARIABLES * NODES))))
            rate[...] = jnp.broadcast_to(jnp.max(rates, axis=1, keepdims=True), rate.shape)

        chosen = dot(table[...], send_route[...])
        chosen = chosen[0:ROWS, :] + chosen[ROWS : 2 * ROWS, :]
        row_ids = lax.broadcasted_iota(jnp.int32, (ROWS, width), 0)
        chosen = jnp.where(row_ids == RATE_ROW, rate[0:1, 0:1], chosen)
        outbox[now] = chosen.T

        for count, chosen_now in sends(step, phase):

            @pl.when(chosen_now)
            def _(count=count):
                for there in order:
                    peer = there[0] * span + there[1]
                    pltpu.make_async_remote_copy(
                        src_ref=outbox.at[now, pl.ds(pl.multiple_of(peer * slots, slots), count)],
                        dst_ref=inbox.at[now, pl.ds(pl.multiple_of(me * slots, slots), count)],
                        send_sem=send_sem.at[now],
                        recv_sem=recv_sem.at[now],
                        device_id=there,
                        device_id_type=pl.DeviceIdType.MESH,
                    ).start()

        mine = pl.ds(pl.multiple_of(me * slots, slots), slots)
        inbox[now, mine, :] = outbox[now, mine, :]

        for face in range(FACES):
            lanes = slice(face * local, (face + 1) * local)
            near[:, lanes] = dot(table[...], route[0:columns, lanes]).astype(BF16)
        for v in range(VARIABLES):
            change[v] = dot(
                vol_wide[...], jnp.concatenate([halves[v], halves[v, 0:PAD, :]], axis=0)
            )

        for count, chosen_now in sends(step, phase):

            @pl.when(chosen_now)
            def _(count=count):
                bulk = inbox.at[now, pl.ds(0, (peers - 1) * count)]
                pltpu.make_async_copy(bulk, bulk, recv_sem.at[now]).wait()

        lane_ids = lax.broadcasted_iota(jnp.int32, (ROWS, width), 1)
        finest = lax.rem(lane_ids, slots) < slot_count(slots, LEVELS - 1)
        brought = jnp.where(jnp.logical_or(now == 1, step == 0), slots, 0)
        received = jnp.where(
            jnp.logical_or(finest, lax.rem(lane_ids, slots) < brought), inbox[now].T, kept[...]
        )
        kept[...] = received

        @pl.when(phase == 0)
        def _():
            fresh = jnp.where(finest[0:1, :], received[RATE_ROW : RATE_ROW + 1, :], 0.0)
            fastest = jnp.max(fresh, axis=1, keepdims=True)
            divisors = jnp.left_shift(1, level_ref[...]).astype(F32)
            coefs[...] = COURANT / fastest / divisors

        received = jnp.where(row_ids == RATE_ROW, 0.0, received)
        high, low = split(received)
        received = jnp.concatenate([high, low], axis=0)

        for face in range(FACES):
            lanes = slice(face * local, (face + 1) * local)
            far = dot(received, route[columns : columns + width, lanes]).astype(BF16)
            near_half[:, lanes] = near[:, lanes] + far

        for g in range(GROUPS):
            parts = []
            for half in range(2):
                rows = slice(half * ROWS + g * GROUP, half * ROWS + (g + 1) * GROUP)
                parts.append(
                    jnp.concatenate(
                        [near_half[rows, f * local : (f + 1) * local] for f in range(FACES)],
                        axis=0,
                    )
                )
            stack = jnp.concatenate([parts[0], parts[0], parts[1]], axis=0)
            lifted[g] = dot(lift_wide[g], stack)

        lowest = jnp.where(
            phase == 0, 0, jnp.where(lax.rem(phase, 4) == 0, 1, jnp.where(lax.rem(phase, 2) == 0, 2, 3))
        )
        scale = jnp.where(level_ref[...] >= lowest, coefs[...], 0.0) * metric_ref[...]
        for base in range(0, PAD, CHUNK):
            rows = slice(base, base + CHUNK)
            combined = [lifted[g, rows, :] - change[g, rows, :] for g in range(GROUPS)]
            last = lifted[0, PAD + base : PAD + base + CHUNK, :]
            for g in range(1, GROUPS):
                last = last + lifted[g, PAD + base : PAD + base + CHUNK, :]
            combined.append(last - change[LAST, rows, :])
            for v in range(VARIABLES):
                mixed = flux_ref[v, 0] * combined[0]
                for w in range(1, VARIABLES):
                    mixed = mixed + flux_ref[v, w] * combined[w]
                moved = fields[v, rows, :] + scale * mixed
                fields[v, rows, :] = moved
                high, low = split(moved)
                halves[v, rows, :] = high
                halves[v, PAD + base : PAD + base + CHUNK, :] = low

        for count, chosen_now in sends(step, phase):

            @pl.when(chosen_now)
            def _(count=count):
                bulk = outbox.at[now, pl.ds(0, (peers - 1) * count)]
                pltpu.make_async_copy(bulk, bulk, send_sem.at[now]).wait()

        return carry

    lax.fori_loop(0, COARSE_STEPS * SUBSTEPS, substep, 0)
    for v in range(VARIABLES):
        out_ref[v] = fields[v, 0:NODES, :]


def body(x, level_map, send_list, face_partner, volume_block, lift_block, flux_mixing, metric_scale):
    peers = lax.axis_size(("wall", "span"))
    span = lax.axis_size("span")
    local = x.shape[2]
    width = send_list.shape[1]
    slots = width // peers
    columns = FACES * local
    vmem = pl.BlockSpec(memory_space=pltpu.VMEM)
    smem = pl.BlockSpec(memory_space=pltpu.SMEM)
    index = index_blocks()
    return pl.pallas_call(
        functools.partial(kernel, peers, span, slots),
        out_shape=jax.ShapeDtypeStruct(x.shape, x.dtype),
        in_specs=[vmem] * 6 + [smem, vmem, pl.BlockSpec(memory_space=pl.ANY)],
        out_specs=vmem,
        scratch_shapes=[
            pltpu.VMEM((VARIABLES, PAD, local), F32),
            pltpu.VMEM((VARIABLES, 2 * PAD, local), BF16),
            pltpu.VMEM((2 * ROWS, columns), BF16),
            pltpu.VMEM((columns + width, columns), BF16),
            pltpu.VMEM((columns, width), BF16),
            pltpu.VMEM((2 * ROWS, columns), BF16),
            pltpu.VMEM((2 * ROWS, columns), BF16),
            pltpu.VMEM((VARIABLES, PAD, local), F32),
            pltpu.VMEM((GROUPS, 2 * PAD, local), F32),
            pltpu.VMEM((GROUPS, 2 * PAD, 3 * STACK), BF16),
            pltpu.VMEM((PAD, 3 * PAD), BF16),
            pltpu.VMEM((PAD, PAD), F32),
            pltpu.VMEM((2 * PAD, PAD), F32),
            pltpu.VMEM((1, local), F32),
            pltpu.VMEM((8, 128), F32),
            pltpu.VMEM(index.shape, BF16),
            pltpu.VMEM((2, width, ROWS), F32),
            pltpu.VMEM((2, width, ROWS), F32),
            pltpu.VMEM((ROWS, width), F32),
            pltpu.SemaphoreType.DMA((2,)),
            pltpu.SemaphoreType.DMA((2,)),
            pltpu.SemaphoreType.DMA,
        ],
        compiler_params=pltpu.CompilerParams(
            collective_id=0, has_side_effects=True, vmem_limit_bytes=60 * 1024 * 1024
        ),
    )(
        x, level_map.reshape(1, local), send_list, face_partner, volume_block, lift_block.T,
        flux_mixing, metric_scale.reshape(1, local),
        jnp.asarray(index),
    )


def solution(mesh):
    both = ("wall", "span")
    return jax.shard_map(
        body,
        mesh=mesh,
        in_specs=(
            P(None, None, both), P(both), P(both, None), P(None, both), P(), P(), P(), P(both),
        ),
        out_specs=P(None, None, both),
        check_vma=False,
    )
```

```python
import functools

import jax
import jax.numpy as jnp
import ml_dtypes
import numpy as np
from jax import lax
from jax.experimental import pallas as pl
from jax.experimental.pallas import tpu as pltpu
from jax.sharding import PartitionSpec as P

VARIABLES = 5
DEGREE = 4
NODES = 125
FACE_NODES = 25
FACES = 6
LEVELS = 4
COARSE_STEPS = 3
SUBSTEPS = 2 ** (LEVELS - 1)
COURANT = 0.6

GROUPS = 4
GROUP = 32
SPARE = GROUP - FACE_NODES
ROWS = GROUPS * GROUP
STACK = FACES * GROUP
RATE_ROW = ROWS - 1
SPREAD = 4
CHUNK = 16
PAD = 128
LAST = VARIABLES - 1

BF16 = jnp.bfloat16
F32 = jnp.float32


def face_nodes():
    cube = np.arange(NODES).reshape(5, 5, 5)
    faces = [cube[0], cube[-1], cube[:, 0], cube[:, -1], cube[:, :, 0], cube[:, :, -1]]
    return np.stack([face.reshape(-1) for face in faces])


def index_blocks():
    nodes = face_nodes()
    pick = np.zeros((GROUPS, STACK, 2 * PAD), np.float32)
    spread = np.zeros((2 * PAD, (GROUPS + 1) * STACK), np.float32)
    own = np.zeros((2 * PAD, PAD), np.float32)
    for face in range(FACES):
        for node in range(FACE_NODES):
            source = face * FACE_NODES + node
            own[source, nodes[face, node]] = 1
            spread[source, face * GROUP + node] = 1
            group, place = divmod(node, SPARE)
            slot = face * GROUP + FACE_NODES + place
            spread[source, (1 + group) * STACK + slot] = 1
            pick[group, slot, PAD + nodes[face, node]] = 1
            for g in range(GROUPS):
                pick[g, face * GROUP + node, nodes[face, node]] = 1
    wide = np.zeros((2 * PAD, SPREAD * 2 * PAD), np.float32)
    wide[:, : spread.shape[1]] = spread
    blocks = [pick.reshape(GROUPS * STACK, 2 * PAD)]
    blocks += [wide[:, i * 2 * PAD : (i + 1) * 2 * PAD] for i in range(SPREAD)]
    blocks.append(np.pad(own, ((0, 0), (0, PAD))))
    return np.concatenate(blocks).astype(ml_dtypes.bfloat16)


def slot_count(slots, lowest):
    def level(k):
        power = 0
        while power < LEVELS - 1 and 2 ** (power + 1) * (slots - k) <= slots:
            power += 1
        return LEVELS - 1 - power

    return sum(level(k) >= lowest for k in range(slots))


def split(x):
    high = x.astype(BF16)
    return high, (x - high.astype(F32)).astype(BF16)


def dot(a, b):
    return jnp.dot(a, b, preferred_element_type=F32)


def kernel(
    peers, span, slots,
    x_ref, level_ref, send_ref, partner_ref, volume_ref, lift_ref, flux_ref, metric_ref,
    index_ref,
    out_ref,
    fields, halves, table, route, send_route, near, far, change, lifted, steady, pairs, pair_near, chosen_lift, chosen, drift, arrived, sent_rows,
    lift_wide, trace_wide, vol_wide, wide, tall, coefs, rate, step_size, index,
    outbox, inbox, kept, send_sem, recv_sem, index_sem,
):
    local = x_ref.shape[2]
    width = peers * slots
    columns = FACES * local
    me = lax.axis_index("wall") * span + lax.axis_index("span")

    def place_of(peer):
        return (peer // span, lax.rem(peer, span))

    index_copy = pltpu.make_async_copy(index_ref, index, index_sem)
    index_copy.start()
    barrier = pltpu.get_barrier_semaphore()

    def greet(i, carry):
        pl.semaphore_signal(
            barrier, inc=1, device_id=place_of(lax.rem(me + i, peers)),
            device_id_type=pl.DeviceIdType.MESH,
        )
        return carry

    lax.fori_loop(1, peers, greet, 0)

    def route_rows(i, carry):
        base = pl.multiple_of(i * 256, 256)
        rows = lax.broadcasted_iota(jnp.int32, (256, local), 0) + base
        for face in range(FACES):
            hit = rows == partner_ref[face : face + 1, :]
            route[pl.ds(base, 256), face * local : (face + 1) * local] = jnp.where(
                hit, 1.0, 0.0
            ).astype(BF16)
        return carry

    lax.fori_loop(0, (columns + width) // 256, route_rows, 0)

    def send_rows(i, carry):
        base = pl.multiple_of(i * 256, 256)
        rows = lax.broadcasted_iota(jnp.int32, (256, width), 0) + base
        send_route[pl.ds(base, 256), :] = jnp.where(rows == send_ref[...], 1.0, 0.0).astype(BF16)
        return carry

    lax.fori_loop(0, columns // 256, send_rows, 0)

    tall[...] = jnp.zeros_like(tall)
    tall[0 : FACES * FACE_NODES, 0:NODES] = lift_ref[...]
    index_copy.wait()
    wide_halves = split(tall[...].T)
    first = GROUPS * STACK
    for place, half in ((0, 0), (1, 1), (2, 0)):
        spread = jnp.concatenate(
            [
                dot(wide_halves[half], index[first + i * 2 * PAD : first + (i + 1) * 2 * PAD, :])
                for i in range(SPREAD)
            ],
            axis=1,
        ).astype(BF16)
        lanes = slice(place * STACK, (place + 1) * STACK)
        for g in range(GROUPS):
            lift_wide[g, 0:PAD, lanes] = spread[:, 0:STACK]
            lift_wide[g, PAD : 2 * PAD, lanes] = spread[:, (1 + g) * STACK : (2 + g) * STACK]
    nodes_of_faces = index[0:STACK, 0:PAD]
    for g in range(GROUPS):
        for part in range(2):
            trace_wide[g, part * STACK : (part + 1) * STACK, :] = dot(
                nodes_of_faces, lift_wide[g, part * PAD : (part + 1) * PAD, :]
            ).astype(BF16)
    own_ref = index[first + SPREAD * 2 * PAD :, 0:PAD]
    own = dot(wide_halves[0], own_ref) + dot(wide_halves[1], own_ref)
    wide[...] = jnp.zeros_like(wide)
    wide[0:NODES, 0:NODES] = volume_ref[...]
    high, low = split(wide[...] + own)
    vol_wide[:, 0:PAD] = high
    vol_wide[:, PAD : 2 * PAD] = high
    vol_wide[:, 2 * PAD : 3 * PAD] = low

    fields[...] = jnp.zeros_like(fields)
    for v in range(VARIABLES):
        fields[v, 0:NODES, :] = x_ref[v]
        high, low = split(fields[v])
        halves[v, 0:PAD, :] = high
        halves[v, PAD : 2 * PAD, :] = low
    rate[...] = jnp.zeros_like(rate)
    kept[...] = jnp.zeros_like(kept)

    element = lax.rem(send_ref[...], local)
    of_sent = jnp.where(
        lax.broadcasted_iota(jnp.int32, (local, width), 0) == element, 1.0, 0.0
    ).astype(BF16)
    metric = metric_ref[...]
    top, rest = split(metric)
    rest_f32 = metric - top.astype(F32)
    bottom = (rest_f32 - rest.astype(F32)).astype(BF16)
    pieces = [top, rest, bottom, level_ref[...].astype(F32).astype(BF16)]
    stacked = jnp.concatenate([jnp.broadcast_to(p.astype(F32), (8, local)) for p in pieces], axis=0)
    gathered = dot(stacked.astype(BF16), of_sent)
    sent_rows[0:1, :] = gathered[0:1, :] + gathered[8:9, :] + gathered[16:17, :]
    sent_rows[1:2, :] = gathered[24:25, :]
    share = jnp.ones((1, width), F32)
    for level in range(1, LEVELS):
        share = jnp.where(gathered[24:25, :] > level - 0.5, 0.5**level, share)
    sent_rows[2:3, :] = share
    for face in range(FACES):
        pairs[:, face * width : (face + 1) * width] = dot(
            route[columns : columns + width, face * local : (face + 1) * local], of_sent
        ).astype(BF16)

    pl.semaphore_wait(barrier, peers - 1)

    walls = peers // span
    my_wall, my_span = lax.axis_index("wall"), lax.axis_index("span")
    order = []
    for ahead in sorted(range(walls), key=lambda w: -min(w, walls - w)):
        wall = my_wall + ahead
        wall = jnp.where(wall >= walls, wall - walls, wall)
        for beside in range(span):
            if ahead or beside:
                other = my_span + beside
                order.append((wall, jnp.where(other >= span, other - span, other)))

    fine, middle = slot_count(slots, LEVELS - 1), slot_count(slots, LEVELS - 2)

    def sends(step, phase):
        first = step == 0
        odd = lax.rem(phase, 2) == 1
        part = jnp.logical_and(odd, lax.rem(phase, 4) == 3)
        whole = jnp.logical_or(first, jnp.logical_and(odd, lax.rem(phase, 4) == 1))
        few = jnp.logical_and(lax.rem(phase, 2) == 0, step > 0)
        return ((fine, few), (middle, part), (slots, whole))

    row_ids = lax.broadcasted_iota(jnp.int32, (ROWS, width), 0)
    lane_ids = lax.broadcasted_iota(jnp.int32, (ROWS, width), 1)

    def make_table():
        for g in range(GROUPS):
            for half in range(2):
                rows = slice(half * PAD, (half + 1) * PAD)
                both = jnp.concatenate([halves[g, rows, :], halves[LAST, rows, :]], axis=0)
                traces = dot(index[g * STACK : (g + 1) * STACK, :], both).astype(BF16)
                for face in range(FACES):
                    table[
                        half * ROWS + g * GROUP : half * ROWS + (g + 1) * GROUP,
                        face * local : (face + 1) * local,
                    ] = traces[face * GROUP : (face + 1) * GROUP, :]

    def choose():
        both = dot(table[...], send_route[...])
        return both[0:ROWS, :] + both[ROWS : 2 * ROWS, :]

    def stacked_halves(ref, g, count):
        parts = [
            jnp.concatenate(
                [
                    ref[
                        half * ROWS + g * GROUP : half * ROWS + (g + 1) * GROUP,
                        f * count : (f + 1) * count,
                    ]
                    for f in range(FACES)
                ],
                axis=0,
            )
            for half in range(2)
        ]
        return jnp.concatenate([parts[0], parts[0], parts[1]], axis=0)

    def mix(values, v):
        mixed = flux_ref[v, 0] * values[0]
        for w in range(1, VARIABLES):
            mixed = mixed + flux_ref[v, w] * values[w]
        return mixed

    def lifted_rows(base):
        values = [lifted[g, base : base + CHUNK, :] for g in range(GROUPS)]
        last = lifted[0, PAD + base : PAD + base + CHUNK, :]
        for g in range(1, GROUPS):
            last = last + lifted[g, PAD + base : PAD + base + CHUNK, :]
        return values + [last]

    def store_halves(v, base, value):
        high, low = split(value)
        halves[v, base : base + CHUNK, :] = high
        halves[v, PAD + base : PAD + base + CHUNK, :] = low

    def set_rate():
        total = jnp.zeros((1, local), F32)
        for v in range(VARIABLES):
            total = total + jnp.sum(fields[v] * fields[v], axis=0, keepdims=True)
        rates = metric_ref[...] * (1.0 + jnp.sqrt(total * (1.0 / (VARIABLES * NODES))))
        rate[...] = jnp.broadcast_to(jnp.max(rates, axis=1, keepdims=True), rate.shape)

    def start_sends(step):
        phase = lax.rem(step, SUBSTEPS)
        now = lax.rem(step, 2)
        outbox[now] = jnp.where(row_ids == RATE_ROW, rate[0:1, 0:1], chosen[...]).T
        for count, chosen_now in sends(step, phase):

            @pl.when(chosen_now)
            def _(count=count):
                for there in order:
                    peer = there[0] * span + there[1]
                    pltpu.make_async_remote_copy(
                        src_ref=outbox.at[now, pl.ds(pl.multiple_of(peer * slots, slots), count)],
                        dst_ref=inbox.at[now, pl.ds(pl.multiple_of(me * slots, slots), count)],
                        send_sem=send_sem.at[now],
                        recv_sem=recv_sem.at[now],
                        device_id=there,
                        device_id_type=pl.DeviceIdType.MESH,
                    ).start()

        mine = pl.ds(pl.multiple_of(me * slots, slots), slots)
        inbox[now, mine, :] = outbox[now, mine, :]

    def local_part():
        for face in range(FACES):
            lanes = slice(face * local, (face + 1) * local)
            near[:, lanes] = dot(table[...], route[0:columns, lanes]).astype(BF16)
        for v in range(VARIABLES):
            change[v] = dot(
                vol_wide[...], jnp.concatenate([halves[v], halves[v, 0:PAD, :]], axis=0)
            )
        for g in range(GROUPS):
            lifted[g] = dot(lift_wide[g], stacked_halves(near, g, local))
        for base in range(0, PAD, CHUNK):
            rows = slice(base, base + CHUNK)
            values = lifted_rows(base)
            values = [values[v] - change[v, rows, :] for v in range(VARIABLES)]
            for v in range(VARIABLES):
                mixed = mix(values, v)
                steady[v, rows, :] = mixed
                store_halves(v, base, mixed)
        make_table()
        drift[...] = choose()

    def substep(step, carry):
        phase = lax.rem(step, SUBSTEPS)
        now = lax.rem(step, 2)
        for count, chosen_now in sends(step, phase):

            @pl.when(chosen_now)
            def _(count=count):
                bulk = inbox.at[now, pl.ds(0, (peers - 1) * count)]
                pltpu.make_async_copy(bulk, bulk, recv_sem.at[now]).wait()

        finest = lax.rem(lane_ids, slots) < slot_count(slots, LEVELS - 1)
        brought = jnp.where(jnp.logical_or(now == 1, step == 0), slots, 0)
        received = jnp.where(
            jnp.logical_or(finest, lax.rem(lane_ids, slots) < brought), inbox[now].T, kept[...]
        )
        kept[...] = received

        @pl.when(phase == 0)
        def _():
            fresh = jnp.where(finest[0:1, :], received[RATE_ROW : RATE_ROW + 1, :], 0.0)
            step_size[...] = jnp.broadcast_to(
                COURANT / jnp.max(fresh, axis=1, keepdims=True), step_size.shape
            )
            divisors = jnp.left_shift(1, level_ref[...]).astype(F32)
            coefs[...] = step_size[0:1, 0:1] / divisors

        received = jnp.where(row_ids == RATE_ROW, 0.0, received)
        high, low = split(received)
        arrived[0:ROWS, :] = high
        arrived[ROWS : 2 * ROWS, :] = low

        lowest = jnp.where(
            phase == 0, 0, jnp.where(lax.rem(phase, 4) == 0, 1, jnp.where(lax.rem(phase, 2) == 0, 2, 3))
        )

        for face in range(FACES):
            lanes = slice(face * width, (face + 1) * width)
            pair_near[:, lanes] = dot(arrived[...], pairs[:, lanes]).astype(BF16)
        for g in range(GROUPS):
            chosen_lift[g] = dot(trace_wide[g], stacked_halves(pair_near, g, width))
        sent_face = lax.div(send_ref[...], local)

        def at_face(take):
            total = jnp.zeros((GROUP, width), F32)
            for face in range(FACES):
                total = jnp.where(sent_face == face, take(face * GROUP), total)
            return total

        values = [at_face(lambda row, g=g: chosen_lift[g, row : row + GROUP, :]) for g in range(GROUPS)]

        def last_rows(row):
            total = chosen_lift[0, STACK + row : STACK + row + GROUP, :]
            for g in range(1, GROUPS):
                total = total + chosen_lift[g, STACK + row : STACK + row + GROUP, :]
            return total

        values.append(at_face(last_rows))
        last = mix(values, LAST)
        spare = lax.broadcasted_iota(jnp.int32, (GROUP, width), 0) >= FACE_NODES
        sent_level = sent_rows[1:2, :]
        sent_scale = jnp.where(
            sent_level >= lowest.astype(F32),
            step_size[0:1, 0:1] * sent_rows[2:3, :],
            0.0,
        ) * sent_rows[0:1, :]
        for g in range(GROUPS):
            rows = slice(g * GROUP, (g + 1) * GROUP)
            moved = pltpu.roll(last, FACE_NODES - SPARE * g, 0)
            packed = jnp.where(spare, moved, mix(values, g))
            chosen[rows, :] = chosen[rows, :] + sent_scale * (drift[rows, :] + packed)

        for count, chosen_now in sends(step, phase):

            @pl.when(chosen_now)
            def _(count=count):
                bulk = outbox.at[now, pl.ds(0, (peers - 1) * count)]
                pltpu.make_async_copy(bulk, bulk, send_sem.at[now]).wait()

        more = step + 1 < steps
        renew = lax.rem(step + 1, SUBSTEPS) == 0

        @pl.when(jnp.logical_and(more, jnp.logical_not(renew)))
        def _():
            start_sends(step + 1)

        for face in range(FACES):
            lanes = slice(face * local, (face + 1) * local)
            far[:, lanes] = dot(arrived[...], route[columns : columns + width, lanes]).astype(BF16)
        for g in range(GROUPS):
            lifted[g] = dot(lift_wide[g], stacked_halves(far, g, local))
        scale = jnp.where(level_ref[...] >= lowest, coefs[...], 0.0) * metric_ref[...]
        for base in range(0, PAD, CHUNK):
            rows = slice(base, base + CHUNK)
            values = lifted_rows(base)
            for v in range(VARIABLES):
                moved = fields[v, rows, :] + scale * (steady[v, rows, :] + mix(values, v))
                fields[v, rows, :] = moved
                store_halves(v, base, moved)

        @pl.when(more)
        def _():
            make_table()

            @pl.when(renew)
            def _():
                set_rate()
                chosen[...] = choose()
                start_sends(step + 1)

            local_part()

        return carry

    steps = COARSE_STEPS * SUBSTEPS
    make_table()
    set_rate()
    chosen[...] = choose()
    start_sends(0)
    local_part()
    lax.fori_loop(0, steps, substep, 0)
    for v in range(VARIABLES):
        out_ref[v] = fields[v, 0:NODES, :]


def body(x, level_map, send_list, face_partner, volume_block, lift_block, flux_mixing, metric_scale):
    peers = lax.axis_size(("wall", "span"))
    span = lax.axis_size("span")
    local = x.shape[2]
    width = send_list.shape[1]
    slots = width // peers
    columns = FACES * local
    vmem = pl.BlockSpec(memory_space=pltpu.VMEM)
    smem = pl.BlockSpec(memory_space=pltpu.SMEM)
    index = index_blocks()
    return pl.pallas_call(
        functools.partial(kernel, peers, span, slots),
        out_shape=jax.ShapeDtypeStruct(x.shape, x.dtype),
        in_specs=[vmem] * 6 + [smem, vmem, pl.BlockSpec(memory_space=pl.ANY)],
        out_specs=vmem,
        scratch_shapes=[
            pltpu.VMEM((VARIABLES, PAD, local), F32),
            pltpu.VMEM((VARIABLES, 2 * PAD, local), BF16),
            pltpu.VMEM((2 * ROWS, columns), BF16),
            pltpu.VMEM((columns + width, columns), BF16),
            pltpu.VMEM((columns, width), BF16),
            pltpu.VMEM((2 * ROWS, columns), BF16),
            pltpu.VMEM((2 * ROWS, columns), BF16),
            pltpu.VMEM((VARIABLES, PAD, local), F32),
            pltpu.VMEM((GROUPS, 2 * PAD, local), F32),
            pltpu.VMEM((VARIABLES, PAD, local), F32),
            pltpu.VMEM((width, FACES * width), BF16),
            pltpu.VMEM((2 * ROWS, FACES * width), BF16),
            pltpu.VMEM((GROUPS, 2 * STACK, width), F32),
            pltpu.VMEM((ROWS, width), F32),
            pltpu.VMEM((ROWS, width), F32),
            pltpu.VMEM((2 * ROWS, width), BF16),
            pltpu.VMEM((8, width), F32),
            pltpu.VMEM((GROUPS, 2 * PAD, 3 * STACK), BF16),
            pltpu.VMEM((GROUPS, 2 * STACK, 3 * STACK), BF16),
            pltpu.VMEM((PAD, 3 * PAD), BF16),
            pltpu.VMEM((PAD, PAD), F32),
            pltpu.VMEM((2 * PAD, PAD), F32),
            pltpu.VMEM((1, local), F32),
            pltpu.VMEM((8, 128), F32),
            pltpu.VMEM((8, 128), F32),
            pltpu.VMEM(index.shape, BF16),
            pltpu.VMEM((2, width, ROWS), F32),
            pltpu.VMEM((2, width, ROWS), F32),
            pltpu.VMEM((ROWS, width), F32),
            pltpu.SemaphoreType.DMA((2,)),
            pltpu.SemaphoreType.DMA((2,)),
            pltpu.SemaphoreType.DMA,
        ],
        compiler_params=pltpu.CompilerParams(
            collective_id=0, has_side_effects=True, vmem_limit_bytes=56 * 1024 * 1024
        ),
    )(
        x, level_map.reshape(1, local), send_list, face_partner, volume_block, lift_block.T,
        flux_mixing, metric_scale.reshape(1, local),
        jnp.asarray(index),
    )


def solution(mesh):
    both = ("wall", "span")
    return jax.shard_map(
        body,
        mesh=mesh,
        in_specs=(
            P(None, None, both), P(both), P(both, None), P(None, both), P(), P(), P(), P(both),
        ),
        out_specs=P(None, None, both),
        check_vma=False,
    )
```

```python
import functools

import jax
import jax.numpy as jnp
import ml_dtypes
import numpy as np
from jax import lax
from jax.experimental import pallas as pl
from jax.experimental.pallas import tpu as pltpu
from jax.sharding import PartitionSpec as P

VARIABLES = 5
DEGREE = 4
NODES = 125
FACE_NODES = 25
FACES = 6
LEVELS = 4
COARSE_STEPS = 3
SUBSTEPS = 2 ** (LEVELS - 1)
COURANT = 0.6

GROUPS = 4
GROUP = 32
SPARE = GROUP - FACE_NODES
ROWS = GROUPS * GROUP
STACK = FACES * GROUP
RATE_ROW = ROWS - 1
SPREAD = 4
CHUNK = 16
PAD = 128
LAST = VARIABLES - 1

BF16 = jnp.bfloat16
F32 = jnp.float32


def face_nodes():
    cube = np.arange(NODES).reshape(5, 5, 5)
    faces = [cube[0], cube[-1], cube[:, 0], cube[:, -1], cube[:, :, 0], cube[:, :, -1]]
    return np.stack([face.reshape(-1) for face in faces])


def index_blocks():
    nodes = face_nodes()
    pick = np.zeros((GROUPS, STACK, 2 * PAD), np.float32)
    spread = np.zeros((2 * PAD, (GROUPS + 1) * STACK), np.float32)
    own = np.zeros((2 * PAD, PAD), np.float32)
    for face in range(FACES):
        for node in range(FACE_NODES):
            source = face * FACE_NODES + node
            own[source, nodes[face, node]] = 1
            spread[source, face * GROUP + node] = 1
            group, place = divmod(node, SPARE)
            slot = face * GROUP + FACE_NODES + place
            spread[source, (1 + group) * STACK + slot] = 1
            pick[group, slot, PAD + nodes[face, node]] = 1
            for g in range(GROUPS):
                pick[g, face * GROUP + node, nodes[face, node]] = 1
    wide = np.zeros((2 * PAD, SPREAD * 2 * PAD), np.float32)
    wide[:, : spread.shape[1]] = spread
    blocks = [pick.reshape(GROUPS * STACK, 2 * PAD)]
    blocks += [wide[:, i * 2 * PAD : (i + 1) * 2 * PAD] for i in range(SPREAD)]
    blocks.append(np.pad(own, ((0, 0), (0, PAD))))
    return np.concatenate(blocks).astype(ml_dtypes.bfloat16)


def slot_count(slots, lowest):
    def level(k):
        power = 0
        while power < LEVELS - 1 and 2 ** (power + 1) * (slots - k) <= slots:
            power += 1
        return LEVELS - 1 - power

    return sum(level(k) >= lowest for k in range(slots))


def split(x):
    high = x.astype(BF16)
    return high, (x - high.astype(F32)).astype(BF16)


def dot(a, b):
    return jnp.dot(a, b, preferred_element_type=F32)


def kernel(
    peers, span, slots,
    x_ref, level_ref, send_ref, partner_ref, volume_ref, lift_ref, flux_ref, metric_ref,
    index_ref,
    out_ref,
    fields, halves, table, tall_table, route, own_route, send_route, near, far, change, lifted, steady, pairs, pair_near, chosen_lift, chosen, drift, arrived, sent_rows,
    lift_wide, trace_wide, vol_wide, wide, tall, coefs, rate, step_size, index,
    outbox, inbox, kept, send_sem, recv_sem, index_sem,
):
    local = x_ref.shape[2]
    width = peers * slots
    columns = FACES * local
    me = lax.axis_index("wall") * span + lax.axis_index("span")

    def place_of(peer):
        return (peer // span, lax.rem(peer, span))

    index_copy = pltpu.make_async_copy(index_ref, index, index_sem)
    index_copy.start()
    barrier = pltpu.get_barrier_semaphore()

    def greet(i, carry):
        pl.semaphore_signal(
            barrier, inc=1, device_id=place_of(lax.rem(me + i, peers)),
            device_id_type=pl.DeviceIdType.MESH,
        )
        return carry

    lax.fori_loop(1, peers, greet, 0)

    for base in range(0, width, 256):
        rows = lax.broadcasted_iota(jnp.int32, (256, local), 0) + (columns + base)
        for face in range(FACES):
            hit = rows == partner_ref[face : face + 1, :]
            route[base : base + 256, face * local : (face + 1) * local] = jnp.where(
                hit, 1.0, 0.0
            ).astype(BF16)
    for face in range(FACES):
        pointers = jnp.broadcast_to(partner_ref[face : face + 1, :], (128, local)).T[:, 0:1]
        for base in range(0, columns, 256):
            lanes = lax.broadcasted_iota(jnp.int32, (local, 256), 1) + base
            own_route[face * local : (face + 1) * local, base : base + 256] = jnp.where(
                lanes == pointers, 1.0, 0.0
            ).astype(BF16)

    def send_rows(i, carry):
        base = pl.multiple_of(i * 256, 256)
        rows = lax.broadcasted_iota(jnp.int32, (256, width), 0) + base
        send_route[pl.ds(base, 256), :] = jnp.where(rows == send_ref[...], 1.0, 0.0).astype(BF16)
        return carry

    lax.fori_loop(0, columns // 256, send_rows, 0)

    tall[...] = jnp.zeros_like(tall)
    tall[0 : FACES * FACE_NODES, 0:NODES] = lift_ref[...]
    index_copy.wait()
    wide_halves = split(tall[...].T)
    first = GROUPS * STACK
    for place, half in ((0, 0), (1, 1), (2, 0)):
        spread = jnp.concatenate(
            [
                dot(wide_halves[half], index[first + i * 2 * PAD : first + (i + 1) * 2 * PAD, :])
                for i in range(SPREAD)
            ],
            axis=1,
        ).astype(BF16)
        lanes = slice(place * STACK, (place + 1) * STACK)
        for g in range(GROUPS):
            lift_wide[g, 0:PAD, lanes] = spread[:, 0:STACK]
            lift_wide[g, PAD : 2 * PAD, lanes] = spread[:, (1 + g) * STACK : (2 + g) * STACK]
    nodes_of_faces = index[0:STACK, 0:PAD]
    for g in range(GROUPS):
        for part in range(2):
            trace_wide[g, part * STACK : (part + 1) * STACK, :] = dot(
                nodes_of_faces, lift_wide[g, part * PAD : (part + 1) * PAD, :]
            ).astype(BF16)
    own_ref = index[first + SPREAD * 2 * PAD :, 0:PAD]
    own = dot(wide_halves[0], own_ref) + dot(wide_halves[1], own_ref)
    wide[...] = jnp.zeros_like(wide)
    wide[0:NODES, 0:NODES] = volume_ref[...]
    high, low = split(wide[...] + own)
    vol_wide[:, 0:PAD] = high
    vol_wide[:, PAD : 2 * PAD] = high
    vol_wide[:, 2 * PAD : 3 * PAD] = low

    fields[...] = jnp.zeros_like(fields)
    for v in range(VARIABLES):
        fields[v, 0:NODES, :] = x_ref[v]
        high, low = split(fields[v])
        halves[v, 0:PAD, :] = high
        halves[v, PAD : 2 * PAD, :] = low
    rate[...] = jnp.zeros_like(rate)
    kept[...] = jnp.zeros_like(kept)

    element = lax.rem(send_ref[...], local)
    of_sent = jnp.where(
        lax.broadcasted_iota(jnp.int32, (local, width), 0) == element, 1.0, 0.0
    ).astype(BF16)
    metric = metric_ref[...]
    top, rest = split(metric)
    rest_f32 = metric - top.astype(F32)
    bottom = (rest_f32 - rest.astype(F32)).astype(BF16)
    pieces = [top, rest, bottom, level_ref[...].astype(F32).astype(BF16)]
    stacked = jnp.concatenate([jnp.broadcast_to(p.astype(F32), (8, local)) for p in pieces], axis=0)
    gathered = dot(stacked.astype(BF16), of_sent)
    sent_rows[0:1, :] = gathered[0:1, :] + gathered[8:9, :] + gathered[16:17, :]
    sent_rows[1:2, :] = gathered[24:25, :]
    share = jnp.ones((1, width), F32)
    for level in range(1, LEVELS):
        share = jnp.where(gathered[24:25, :] > level - 0.5, 0.5**level, share)
    sent_rows[2:3, :] = share
    for face in range(FACES):
        pairs[:, face * width : (face + 1) * width] = dot(
            route[:, face * local : (face + 1) * local], of_sent
        ).astype(BF16)

    pl.semaphore_wait(barrier, peers - 1)

    walls = peers // span
    my_wall, my_span = lax.axis_index("wall"), lax.axis_index("span")
    order = []
    for ahead in sorted(range(walls), key=lambda w: -min(w, walls - w)):
        wall = my_wall + ahead
        wall = jnp.where(wall >= walls, wall - walls, wall)
        for beside in range(span):
            if ahead or beside:
                other = my_span + beside
                order.append((wall, jnp.where(other >= span, other - span, other)))

    fine, middle = slot_count(slots, LEVELS - 1), slot_count(slots, LEVELS - 2)

    def sends(step, phase):
        first = step == 0
        odd = lax.rem(phase, 2) == 1
        part = jnp.logical_and(odd, lax.rem(phase, 4) == 3)
        whole = jnp.logical_or(first, jnp.logical_and(odd, lax.rem(phase, 4) == 1))
        few = jnp.logical_and(lax.rem(phase, 2) == 0, step > 0)
        return ((fine, few), (middle, part), (slots, whole))

    row_ids = lax.broadcasted_iota(jnp.int32, (ROWS, width), 0)
    lane_ids = lax.broadcasted_iota(jnp.int32, (ROWS, width), 1)

    def make_table():
        for g in range(GROUPS):
            for half in range(2):
                rows = slice(half * PAD, (half + 1) * PAD)
                both = jnp.concatenate([halves[g, rows, :], halves[LAST, rows, :]], axis=0)
                traces = dot(index[g * STACK : (g + 1) * STACK, :], both).astype(BF16)
                for face in range(FACES):
                    table[
                        half * ROWS + g * GROUP : half * ROWS + (g + 1) * GROUP,
                        face * local : (face + 1) * local,
                    ] = traces[face * GROUP : (face + 1) * GROUP, :]

    def choose():
        both = dot(table[...], send_route[...])
        return both[0:ROWS, :] + both[ROWS : 2 * ROWS, :]

    def stacked_halves(ref, g, count):
        parts = [
            jnp.concatenate(
                [
                    ref[
                        half * ROWS + g * GROUP : half * ROWS + (g + 1) * GROUP,
                        f * count : (f + 1) * count,
                    ]
                    for f in range(FACES)
                ],
                axis=0,
            )
            for half in range(2)
        ]
        return jnp.concatenate([parts[0], parts[0], parts[1]], axis=0)

    def mix(values, v):
        mixed = flux_ref[v, 0] * values[0]
        for w in range(1, VARIABLES):
            mixed = mixed + flux_ref[v, w] * values[w]
        return mixed

    def lifted_rows(base):
        values = [lifted[g, base : base + CHUNK, :] for g in range(GROUPS)]
        last = lifted[0, PAD + base : PAD + base + CHUNK, :]
        for g in range(1, GROUPS):
            last = last + lifted[g, PAD + base : PAD + base + CHUNK, :]
        return values + [last]

    def store_halves(v, base, value):
        high, low = split(value)
        halves[v, base : base + CHUNK, :] = high
        halves[v, PAD + base : PAD + base + CHUNK, :] = low

    def set_rate():
        total = jnp.zeros((1, local), F32)
        for v in range(VARIABLES):
            total = total + jnp.sum(fields[v] * fields[v], axis=0, keepdims=True)
        rates = metric_ref[...] * (1.0 + jnp.sqrt(total * (1.0 / (VARIABLES * NODES))))
        rate[...] = jnp.broadcast_to(jnp.max(rates, axis=1, keepdims=True), rate.shape)

    def start_sends(step):
        phase = lax.rem(step, SUBSTEPS)
        now = lax.rem(step, 2)
        outbox[now] = jnp.where(row_ids == RATE_ROW, rate[0:1, 0:1], chosen[...]).T
        for count, chosen_now in sends(step, phase):

            @pl.when(chosen_now)
            def _(count=count):
                for there in order:
                    peer = there[0] * span + there[1]
                    pltpu.make_async_remote_copy(
                        src_ref=outbox.at[now, pl.ds(pl.multiple_of(peer * slots, slots), count)],
                        dst_ref=inbox.at[now, pl.ds(pl.multiple_of(me * slots, slots), count)],
                        send_sem=send_sem.at[now],
                        recv_sem=recv_sem.at[now],
                        device_id=there,
                        device_id_type=pl.DeviceIdType.MESH,
                    ).start()

        mine = pl.ds(pl.multiple_of(me * slots, slots), slots)
        inbox[now, mine, :] = outbox[now, mine, :]

    def local_part():
        for face in range(FACES):
            lanes = slice(face * local, (face + 1) * local)
            tall_table[lanes, :] = table[:, lanes].T
        found = dot(own_route[...], tall_table[...])
        for face in range(FACES):
            lanes = slice(face * local, (face + 1) * local)
            near[:, lanes] = found[lanes, :].astype(BF16).T
        for v in range(VARIABLES):
            change[v] = dot(
                vol_wide[...], jnp.concatenate([halves[v], halves[v, 0:PAD, :]], axis=0)
            )
        for g in range(GROUPS):
            lifted[g] = dot(lift_wide[g], stacked_halves(near, g, local))
        for base in range(0, PAD, CHUNK):
            rows = slice(base, base + CHUNK)
            values = lifted_rows(base)
            values = [values[v] - change[v, rows, :] for v in range(VARIABLES)]
            for v in range(VARIABLES):
                mixed = mix(values, v)
                steady[v, rows, :] = mixed
                store_halves(v, base, mixed)
        make_table()
        drift[...] = choose()

    def substep(step, carry):
        phase = lax.rem(step, SUBSTEPS)
        now = lax.rem(step, 2)
        for count, chosen_now in sends(step, phase):

            @pl.when(chosen_now)
            def _(count=count):
                bulk = inbox.at[now, pl.ds(0, (peers - 1) * count)]
                pltpu.make_async_copy(bulk, bulk, recv_sem.at[now]).wait()

        finest = lax.rem(lane_ids, slots) < slot_count(slots, LEVELS - 1)
        brought = jnp.where(jnp.logical_or(now == 1, step == 0), slots, 0)
        received = jnp.where(
            jnp.logical_or(finest, lax.rem(lane_ids, slots) < brought), inbox[now].T, kept[...]
        )
        kept[...] = received

        @pl.when(phase == 0)
        def _():
            fresh = jnp.where(finest[0:1, :], received[RATE_ROW : RATE_ROW + 1, :], 0.0)
            step_size[...] = jnp.broadcast_to(
                COURANT / jnp.max(fresh, axis=1, keepdims=True), step_size.shape
            )
            divisors = jnp.left_shift(1, level_ref[...]).astype(F32)
            coefs[...] = step_size[0:1, 0:1] / divisors

        received = jnp.where(row_ids == RATE_ROW, 0.0, received)
        high, low = split(received)
        arrived[0:ROWS, :] = high
        arrived[ROWS : 2 * ROWS, :] = low

        lowest = jnp.where(
            phase == 0, 0, jnp.where(lax.rem(phase, 4) == 0, 1, jnp.where(lax.rem(phase, 2) == 0, 2, 3))
        )

        for face in range(FACES):
            lanes = slice(face * width, (face + 1) * width)
            pair_near[:, lanes] = dot(arrived[...], pairs[:, lanes]).astype(BF16)
        for g in range(GROUPS):
            chosen_lift[g] = dot(trace_wide[g], stacked_halves(pair_near, g, width))
        sent_face = lax.div(send_ref[...], local)

        def at_face(take):
            total = jnp.zeros((GROUP, width), F32)
            for face in range(FACES):
                total = jnp.where(sent_face == face, take(face * GROUP), total)
            return total

        values = [at_face(lambda row, g=g: chosen_lift[g, row : row + GROUP, :]) for g in range(GROUPS)]

        def last_rows(row):
            total = chosen_lift[0, STACK + row : STACK + row + GROUP, :]
            for g in range(1, GROUPS):
                total = total + chosen_lift[g, STACK + row : STACK + row + GROUP, :]
            return total

        values.append(at_face(last_rows))
        last = mix(values, LAST)
        spare = lax.broadcasted_iota(jnp.int32, (GROUP, width), 0) >= FACE_NODES
        sent_level = sent_rows[1:2, :]
        sent_scale = jnp.where(
            sent_level >= lowest.astype(F32),
            step_size[0:1, 0:1] * sent_rows[2:3, :],
            0.0,
        ) * sent_rows[0:1, :]
        for g in range(GROUPS):
            rows = slice(g * GROUP, (g + 1) * GROUP)
            moved = pltpu.roll(last, FACE_NODES - SPARE * g, 0)
            packed = jnp.where(spare, moved, mix(values, g))
            chosen[rows, :] = chosen[rows, :] + sent_scale * (drift[rows, :] + packed)

        for count, chosen_now in sends(step, phase):

            @pl.when(chosen_now)
            def _(count=count):
                bulk = outbox.at[now, pl.ds(0, (peers - 1) * count)]
                pltpu.make_async_copy(bulk, bulk, send_sem.at[now]).wait()

        more = step + 1 < steps
        renew = lax.rem(step + 1, SUBSTEPS) == 0

        @pl.when(jnp.logical_and(more, jnp.logical_not(renew)))
        def _():
            start_sends(step + 1)

        for face in range(FACES):
            lanes = slice(face * local, (face + 1) * local)
            far[:, lanes] = dot(arrived[...], route[:, lanes]).astype(BF16)
        for g in range(GROUPS):
            lifted[g] = dot(lift_wide[g], stacked_halves(far, g, local))
        scale = jnp.where(level_ref[...] >= lowest, coefs[...], 0.0) * metric_ref[...]
        for base in range(0, PAD, CHUNK):
            rows = slice(base, base + CHUNK)
            values = lifted_rows(base)
            for v in range(VARIABLES):
                moved = fields[v, rows, :] + scale * (steady[v, rows, :] + mix(values, v))
                fields[v, rows, :] = moved
                store_halves(v, base, moved)

        @pl.when(more)
        def _():
            make_table()

            @pl.when(renew)
            def _():
                set_rate()
                chosen[...] = choose()
                start_sends(step + 1)

            local_part()

        return carry

    steps = COARSE_STEPS * SUBSTEPS
    make_table()
    set_rate()
    chosen[...] = choose()
    start_sends(0)
    local_part()
    lax.fori_loop(0, steps, substep, 0)
    for v in range(VARIABLES):
        out_ref[v] = fields[v, 0:NODES, :]


def body(x, level_map, send_list, face_partner, volume_block, lift_block, flux_mixing, metric_scale):
    peers = lax.axis_size(("wall", "span"))
    span = lax.axis_size("span")
    local = x.shape[2]
    width = send_list.shape[1]
    slots = width // peers
    columns = FACES * local
    vmem = pl.BlockSpec(memory_space=pltpu.VMEM)
    smem = pl.BlockSpec(memory_space=pltpu.SMEM)
    index = index_blocks()
    return pl.pallas_call(
        functools.partial(kernel, peers, span, slots),
        out_shape=jax.ShapeDtypeStruct(x.shape, x.dtype),
        in_specs=[vmem] * 6 + [smem, vmem, pl.BlockSpec(memory_space=pl.ANY)],
        out_specs=vmem,
        scratch_shapes=[
            pltpu.VMEM((VARIABLES, PAD, local), F32),
            pltpu.VMEM((VARIABLES, 2 * PAD, local), BF16),
            pltpu.VMEM((2 * ROWS, columns), BF16),
            pltpu.VMEM((columns, 2 * ROWS), BF16),
            pltpu.VMEM((width, columns), BF16),
            pltpu.VMEM((columns, columns), BF16),
            pltpu.VMEM((columns, width), BF16),
            pltpu.VMEM((2 * ROWS, columns), BF16),
            pltpu.VMEM((2 * ROWS, columns), BF16),
            pltpu.VMEM((VARIABLES, PAD, local), F32),
            pltpu.VMEM((GROUPS, 2 * PAD, local), F32),
            pltpu.VMEM((VARIABLES, PAD, local), F32),
            pltpu.VMEM((width, FACES * width), BF16),
            pltpu.VMEM((2 * ROWS, FACES * width), BF16),
            pltpu.VMEM((GROUPS, 2 * STACK, width), F32),
            pltpu.VMEM((ROWS, width), F32),
            pltpu.VMEM((ROWS, width), F32),
            pltpu.VMEM((2 * ROWS, width), BF16),
            pltpu.VMEM((8, width), F32),
            pltpu.VMEM((GROUPS, 2 * PAD, 3 * STACK), BF16),
            pltpu.VMEM((GROUPS, 2 * STACK, 3 * STACK), BF16),
            pltpu.VMEM((PAD, 3 * PAD), BF16),
            pltpu.VMEM((PAD, PAD), F32),
            pltpu.VMEM((2 * PAD, PAD), F32),
            pltpu.VMEM((1, local), F32),
            pltpu.VMEM((8, 128), F32),
            pltpu.VMEM((8, 128), F32),
            pltpu.VMEM(index.shape, BF16),
            pltpu.VMEM((2, width, ROWS), F32),
            pltpu.VMEM((2, width, ROWS), F32),
            pltpu.VMEM((ROWS, width), F32),
            pltpu.SemaphoreType.DMA((2,)),
            pltpu.SemaphoreType.DMA((2,)),
            pltpu.SemaphoreType.DMA,
        ],
        compiler_params=pltpu.CompilerParams(
            collective_id=0, has_side_effects=True, vmem_limit_bytes=56 * 1024 * 1024
        ),
    )(
        x, level_map.reshape(1, local), send_list, face_partner, volume_block, lift_block.T,
        flux_mixing, metric_scale.reshape(1, local),
        jnp.asarray(index),
    )


def solution(mesh):
    both = ("wall", "span")
    return jax.shard_map(
        body,
        mesh=mesh,
        in_specs=(
            P(None, None, both), P(both), P(both, None), P(None, both), P(), P(), P(), P(both),
        ),
        out_specs=P(None, None, both),
        check_vma=False,
    )
```
